32 devices in a mesh: row: 4 (over x, core), col: 4 (over z), slab: 2 (over y).
Axes of the slice: x: 2, y: 2, z: 4, core: 2. Of those that a mesh axis runs over, the one named last changes fastest.
Arguments:
- fields: bfloat16 [2, 2048, 1024], P(None, ('row', 'col', 'slab')), may hold values from -0.8984375 to 0.8984375
Outputs:
- gram: float32 [2, 2048, 2048], P(None, ('row', 'slab'), 'col')
The draws below stay inside these ranges and needn't reach their ends.
All inputs are finite; a program needn't handle non-finite values.
Results may differ from the reference program's by a relative error of at most 0.01.
Values may be sent and summed in bfloat16 or wider, within the bound.
No kernel may reach another device: no remote copies, remote signals or barrier semaphores. Data moves between devices by JAX's collectives and lax.ppermute only.
A program may use at most 64 MiB of HBM per device.

```python
import jax
import jax.numpy as jnp
from jax import lax

PIX = 1024
NE = 2048
ROWB = 512
KBLOCK = 128
N_ROW = 4
N_COL = 4
N_SLAB = 2


def block_levels(stream_key, shape, split, low, largest):
    loudness, own = 1.0, jax.random.fold_in(stream_key, 6)
    for axis_at, blocks in split:
        steps = jnp.exp(jax.random.uniform(jax.random.fold_in(own, axis_at), (blocks,), jnp.float32, low / len(split), largest / len(split)))
        loudness = loudness * jnp.repeat(steps, shape[axis_at] // blocks).reshape([-1 if axis == axis_at else 1 for axis in range(len(shape))])
    return loudness


def bell_draw(key, dims, width, bound, split=(), held_as=jnp.bfloat16):
    drawn = jax.random.normal(key, dims, jnp.float32) * width
    if len(split) > 0:
        drawn = block_levels(key, dims, split, -0.22, 0.18) * drawn
    return jnp.clip(drawn, min=-bound, max=bound).astype(held_as)


def setup_inputs(seed: int = 0) -> dict:
    key_of = jax.random.split(jax.random.key(seed), 2)
    return {
        "fields": bell_draw(key_of[0], (2, NE, PIX), 0.15, 0.8984375, ((1, 32),)),
    }


def pair_block(left, right):
    real = jnp.dot(left[0], right[0].T, precision=lax.Precision.HIGHEST) + jnp.dot(left[1], right[1].T, precision=lax.Precision.HIGHEST)
    imag = jnp.dot(left[0], right[1].T, precision=lax.Precision.HIGHEST) - jnp.dot(left[1], right[0].T, precision=lax.Precision.HIGHEST)
    return jnp.stack([real, imag])


def reference(fields):
    whole = fields.astype(jnp.float32)
    columns = whole.reshape(2, N_ROW, N_COL, KBLOCK, PIX).transpose(0, 2, 1, 3, 4).reshape(2, NE, PIX)
    half = PIX // N_SLAB
    block_rows = 512 if ROWB % 512 == 0 else ROWB
    blocks = whole.reshape(2, NE // block_rows, block_rows, PIX).transpose(1, 0, 2, 3)

    def one_block(rows_block):
        total = jnp.zeros((2, block_rows, NE), jnp.float32)
        for sub in range(N_SLAB):
            left = rows_block[:, :, sub * half:(sub + 1) * half]
            right = columns[:, :, sub * half:(sub + 1) * half]
            partial_sum = lax.optimization_barrier(pair_block(left, right).astype(jnp.bfloat16))
            total = total + partial_sum.astype(jnp.float32)
        return total

    result = lax.map(one_block, blocks)
    return result.transpose(1, 0, 2, 3).reshape(2, NE, NE)
```

```python
import functools

import jax
import jax.numpy as jnp
from jax import lax
from jax.experimental import pallas as pl
from jax.experimental.pallas import tpu as pltpu
from jax.sharding import PartitionSpec as P

AXES = ("row", "col", "slab")
TILE = 512


def dot(left, right):
    return lax.dot_general(left, right, (((1,), (1,)), ((), ())), preferred_element_type=jnp.float32)


def device_pairs(sizes, target):
    rows, cols, slabs = sizes
    pairs = []
    for r in range(rows):
        for c in range(cols):
            for s in range(slabs):
                to = target(r, c, s)
                if to is not None:
                    pairs.append(((r * cols + c) * slabs + s, (to[0] * cols + to[1]) * slabs + to[2]))
    return pairs


def row_plan(sizes):
    _, cols, _ = sizes
    half = cols // 2
    plan = []
    for shift in list(range(1, half)) + [0]:
        for turn in range(2):
            plan.append((shift if shift > 0 else None, (shift + 1) % half, turn))
    return plan


def row_pairs(sizes, near_shift, far_shift, turn):
    rows, cols, slabs = sizes
    half = cols // 2
    pairs = []
    for r in range(rows):
        for c in range(cols):
            for s in range(slabs):
                near = c // half == s
                shift = near_shift if near else far_shift
                if shift is None:
                    continue
                source = (r, s * half + (c + shift) % half, s ^ turn if near else s ^ turn ^ 1)
                pairs.append(((source[0] * cols + source[1]) * slabs + source[2], (r * cols + c) * slabs + s))
    return pairs


def gram_kernel(sizes, plan, offsets, *refs):
    rows, cols, slabs = sizes
    half = cols // 2
    n_col = len(offsets)
    col_refs = refs[:n_col]
    row_refs = refs[n_col : n_col + len(plan)]
    out_ref, left, right = refs[n_col + len(plan) :]
    r, c, s = (lax.axis_index(axis) for axis in AXES)
    near = lax.div(c, half) == s
    _, size, pixels = col_refs[0].shape

    for ref, (dr, ds) in zip(col_refs, offsets):
        at = pl.multiple_of((lax.bitwise_xor(r, dr) * slabs + lax.bitwise_xor(s, ds)) * size, size)
        right[:, pl.ds(at, size), :] = ref[...]

    for ref, (near_shift, far_shift, turn) in zip(row_refs, plan):
        near_place = lax.rem(c + (near_shift or 0), half) * slabs + lax.bitwise_xor(s, turn)
        far_place = lax.rem(c + far_shift, half) * slabs + lax.bitwise_xor(s, turn ^ 1)
        at = pl.multiple_of(jnp.where(near, near_place, far_place) * size, size)
        block = ref[...]
        if near_shift is None:
            block = jnp.where(near, col_refs[turn][...], block)
        left[:, pl.ds(at, size), :] = block

    @pl.loop(0, right.shape[1] // TILE)
    def _(tile):
        at = pl.multiple_of(tile * TILE, TILE)
        here = pl.ds(at, TILE)
        out_ref[0, :, here] = dot(left[0], right[0, here]) + dot(left[1], right[1, here])
        out_ref[1, :, here] = dot(left[0], right[1, here]) - dot(left[1], right[0, here])


def solution(mesh):
    sizes = tuple(mesh.shape[axis] for axis in AXES)
    rows, cols, slabs = sizes
    plan = row_plan(sizes)

    def body(fields):
        _, size, pixels = fields.shape
        blocks, offsets = [fields], [(0, 0)]
        steps = [(0, 1)]
        bit = rows // 2
        while bit > 0:
            steps.append((bit, 0))
            bit //= 2
        for dr, ds in steps:
            pairs = device_pairs(sizes, lambda r, c, s: (r ^ dr, c, s ^ ds))
            blocks = blocks + [lax.ppermute(block, AXES, pairs) for block in blocks]
            offsets = offsets + [(a ^ dr, b ^ ds) for a, b in offsets]
        row_blocks = [lax.ppermute(fields, AXES, row_pairs(sizes, *step)) for step in plan]
        out_rows = cols // 2 * slabs * size
        out_cols = rows * slabs * size
        return pl.pallas_call(
            functools.partial(gram_kernel, sizes, plan, offsets),
            out_shape=jax.ShapeDtypeStruct((2, out_rows, out_cols), jnp.float32),
            in_specs=[pl.BlockSpec(memory_space=pltpu.VMEM)] * (len(blocks) + len(plan)),
            out_specs=pl.BlockSpec(memory_space=pltpu.VMEM),
            scratch_shapes=[
                pltpu.VMEM((2, out_rows, pixels), jnp.bfloat16),
                pltpu.VMEM((2, out_cols, pixels), jnp.bfloat16),
            ],
            compiler_params=pltpu.CompilerParams(vmem_limit_bytes=32 * 1024 * 1024),
        )(*[pltpu.with_memory_space_constraint(block, pltpu.VMEM) for block in blocks + row_blocks])

    placed = (P(None, AXES, None),)
    return jax.shard_map(
        body, mesh=mesh, in_specs=placed, out_specs=P(None, ("row", "slab"), "col"), check_vma=False
    )
```

```python
import functools

import jax
import jax.numpy as jnp
from jax import lax
from jax.experimental import pallas as pl
from jax.experimental.pallas import tpu as pltpu
from jax.sharding import PartitionSpec as P

AXES = ("row", "col", "slab")
TILE = 256
ANY = pl.BlockSpec(memory_space=pl.ANY)
VMEM = pl.BlockSpec(memory_space=pltpu.VMEM)
PARAMS = pltpu.CompilerParams(vmem_limit_bytes=24 * 1024 * 1024)
EARLY, MIDDLE = 30_000_000_000, 10_000_000_000


def weight(flops):
    return pl.CostEstimate(flops=flops, bytes_accessed=1 << 18, transcendentals=0) if flops else None


def dot(left, right):
    return lax.dot_general(left, right, (((1,), (1,)), ((), ())), preferred_element_type=jnp.float32)


def in_vmem(arrays):
    return [pltpu.with_memory_space_constraint(array, pltpu.VMEM) for array in arrays]


def split_kernel(fields, *refs):
    outs, sems = refs[:-1], refs[-1]
    copies = [pltpu.make_async_copy(fields.at[i], out, sems.at[i]) for i, out in enumerate(outs)]
    for copy in copies:
        copy.start()
    for copy in copies:
        copy.wait()


def choose_kernel(sizes, own, far, keep, give):
    near = lax.div(lax.axis_index("col"), sizes[1] // 2) == lax.axis_index("slab")
    keep[...] = jnp.where(near, own[...], far[...])
    give[...] = jnp.where(near, far[...], own[...])


def order_kernel(sizes, offsets, own_real, own_imag, *refs):
    r, s = lax.axis_index("row"), lax.axis_index("slab")
    cols, mine = refs[:-1], refs[-1]
    size = own_real.shape[0]

    def place(dr, ds):
        at = lax.div(lax.bitwise_xor(r, dr), 2) * sizes[2] + lax.bitwise_xor(s, ds)
        return pl.ds(pl.multiple_of(at * size, size), size)

    for i, own in enumerate((own_real, own_imag)):
        mine[i, place(0, 0)] = own[...]
    for ref, (dr, ds) in zip(cols, offsets[1:]):
        mine[:, place(dr, ds)] = ref[...]


def rows_in_order(sizes, places, refs, left):
    c, s = lax.axis_index("col"), lax.axis_index("slab")
    for ref, (shift, turn) in zip(refs, places):
        size = ref.shape[0]
        at = lax.rem(lax.bitwise_xor(c, shift), sizes[1] // 2) * sizes[2] + lax.bitwise_xor(s, turn)
        left[pl.ds(pl.multiple_of(at * size, size), size)] = ref[...]


def over_columns(sizes, mine, other, step):
    group = mine.shape[1] // (sizes[0] // 2)
    core = lax.rem(lax.axis_index("row"), 2)
    for cols, which in ((mine, core), (other, 1 - core)):

        @pl.loop(0, mine.shape[1] // TILE)
        def _(tile):
            here = pl.ds(pl.multiple_of(tile * TILE, TILE), TILE)
            parts = []
            for i in range(TILE // group):
                at = (2 * (tile * (TILE // group) + i) + which) * group
                parts.append((slice(i * group, (i + 1) * group), pl.ds(pl.multiple_of(at, group), group)))
            step(cols[0, here], cols[1, here], parts)


def real_rows_kernel(sizes, places, mine, other, *refs):
    blocks, out, left = refs[:-2], refs[-2], refs[-1]
    rows_in_order(sizes, places, blocks, left)

    def step(real, imag, parts):
        with_real, with_imag = dot(left[...], real), dot(left[...], imag)
        for part, at in parts:
            out[0, :, at] = with_real[:, part]
            out[1, :, at] = with_imag[:, part]

    over_columns(sizes, mine, other, step)


def imag_rows_kernel(sizes, places, mine, other, so_far, *refs):
    blocks, out, left = refs[:-2], refs[-2], refs[-1]
    rows_in_order(sizes, places, blocks, left)

    def step(real, imag, parts):
        with_real, with_imag = dot(left[...], real), dot(left[...], imag)
        for part, at in parts:
            out[0, :, at] = so_far[0, :, at] + with_imag[:, part]
            out[1, :, at] = so_far[1, :, at] - with_real[:, part]

    over_columns(sizes, mine, other, step)


def solution(mesh):
    sizes = tuple(mesh.shape[axis] for axis in AXES)
    rows, cols, slabs = sizes
    half = cols // 2

    def exchange(array, dr, dc, ds):
        pairs = []
        for r in range(rows):
            for c in range(cols):
                for s in range(slabs):
                    pairs.append(((r * cols + c) * slabs + s, ((r ^ dr) * cols + (c ^ dc)) * slabs + (s ^ ds)))
        return lax.ppermute(array, AXES, pairs)

    def body(fields):
        _, size, pixels = fields.shape
        out_rows, out_cols = half * slabs * size, rows * slabs * size
        part_shape = pltpu.VMEM((size, pixels), fields.dtype)

        def call(kernel, out_shape, arrays, scratch=(), specs=None, flops=0):
            return pl.pallas_call(
                kernel,
                out_shape=out_shape,
                in_specs=specs or [VMEM] * len(arrays),
                out_specs=jax.tree.map(lambda _: VMEM, out_shape),
                scratch_shapes=scratch,
                compiler_params=PARAMS,
                cost_estimate=weight(flops),
            )(*(arrays if specs else in_vmem(arrays)))

        own = call(
            split_kernel, [part_shape] * 2, [pltpu.with_memory_space_constraint(fields, pltpu.HBM)],
            [pltpu.SemaphoreType.DMA((2,))], [ANY],
        )
        blocks, offsets = [fields], [(0, 0)]
        steps = [(0, 1)]
        bit = rows // 2
        while bit > 1:
            steps.append((bit, 0))
            bit //= 2
        for dr, ds in steps:
            blocks = blocks + [exchange(block, dr, 0, ds) for block in blocks]
            offsets = offsets + [(a ^ dr, b ^ ds) for a, b in offsets]
        mine = call(
            functools.partial(order_kernel, sizes, offsets),
            pltpu.VMEM((2, out_cols // 2, pixels), fields.dtype), [*own, *blocks[1:]],
        )
        other = exchange(mine, 1, 0, 0)
        places = [(shift, turn) for shift in range(half) for turn in range(slabs)]
        slots = []
        for part in own:
            far = exchange(part, 0, half, 0)
            keep, give = call(functools.partial(choose_kernel, sizes), [part_shape] * 2, [part, far], flops=EARLY)
            got = [keep]
            for shift, turn in places[1:]:
                got.append(exchange(give if turn else keep, 0, shift, turn))
            slots.append(got)
        left = pltpu.VMEM((out_rows, pixels), fields.dtype)
        so_far = call(
            functools.partial(real_rows_kernel, sizes, places),
            pltpu.VMEM((2, out_rows, out_cols), jnp.float32), [mine, other, *slots[0]], [left], flops=MIDDLE,
        )
        return call(
            functools.partial(imag_rows_kernel, sizes, places),
            jax.ShapeDtypeStruct((2, out_rows, out_cols), jnp.float32), [mine, other, so_far, *slots[1]], [left],
        )

    placed = (P(None, AXES, None),)
    return jax.shard_map(
        body, mesh=mesh, in_specs=placed, out_specs=P(None, ("row", "slab"), "col"), check_vma=False
    )
```

```python
import functools

import jax
import jax.numpy as jnp
from jax import lax
from jax.experimental import pallas as pl
from jax.experimental.pallas import tpu as pltpu
from jax.sharding import PartitionSpec as P

AXES = ("row", "col", "slab")
TILE = 256
ANY = pl.BlockSpec(memory_space=pl.ANY)
VMEM = pl.BlockSpec(memory_space=pltpu.VMEM)
PARAMS = pltpu.CompilerParams(vmem_limit_bytes=24 * 1024 * 1024)
EARLY, MIDDLE = 30_000_000_000, 10_000_000_000


def weight(flops):
    return pl.CostEstimate(flops=flops, bytes_accessed=1 << 18, transcendentals=0) if flops else None


def dot(left, right):
    return lax.dot_general(left, right, (((1,), (1,)), ((), ())), preferred_element_type=jnp.float32)


def in_vmem(arrays):
    return [pltpu.with_memory_space_constraint(array, pltpu.VMEM) for array in arrays]


def split_kernel(fields, *refs):
    outs, sems = refs[:-1], refs[-1]
    copies = [pltpu.make_async_copy(fields.at[i], out, sems.at[i]) for i, out in enumerate(outs)]
    for copy in copies:
        copy.start()
    for copy in copies:
        copy.wait()


def relay_kernel(part, after, out):
    out[...] = part[...]


def choose_kernel(sizes, own, far, keep, give):
    near = lax.div(lax.axis_index("col"), sizes[1] // 2) == lax.axis_index("slab")
    keep[...] = jnp.where(near, own[...], far[...])
    give[...] = jnp.where(near, far[...], own[...])


def order_kernel(sizes, offsets, own_real, own_imag, *refs):
    r, s = lax.axis_index("row"), lax.axis_index("slab")
    cols, mine = refs[:-1], refs[-1]
    size = own_real.shape[0]

    def place(dr, ds):
        at = lax.div(lax.bitwise_xor(r, dr), 2) * sizes[2] + lax.bitwise_xor(s, ds)
        return pl.ds(pl.multiple_of(at * size, size), size)

    for i, own in enumerate((own_real, own_imag)):
        mine[i, place(0, 0)] = own[...]
    for ref, (dr, ds) in zip(cols, offsets[1:]):
        mine[:, place(dr, ds)] = ref[...]


def rows_in_order(sizes, places, refs, left):
    c, s = lax.axis_index("col"), lax.axis_index("slab")
    for ref, (shift, turn) in zip(refs, places):
        size = ref.shape[0]
        at = lax.rem(lax.bitwise_xor(c, shift), sizes[1] // 2) * sizes[2] + lax.bitwise_xor(s, turn)
        left[pl.ds(pl.multiple_of(at * size, size), size)] = ref[...]


def over_columns(sizes, mine, other, step):
    group = mine.shape[1] // (sizes[0] // 2)
    core = lax.rem(lax.axis_index("row"), 2)
    for cols, which in ((mine, core), (other, 1 - core)):

        @pl.loop(0, mine.shape[1] // TILE)
        def _(tile):
            here = pl.ds(pl.multiple_of(tile * TILE, TILE), TILE)
            parts = []
            for i in range(TILE // group):
                at = (2 * (tile * (TILE // group) + i) + which) * group
                parts.append((slice(i * group, (i + 1) * group), pl.multiple_of(at, group)))
            step(cols[0, here], cols[1, here], parts)


def real_rows_kernel(sizes, places, mine, other, *refs):
    blocks, out, left = refs[:-2], refs[-2], refs[-1]
    rows_in_order(sizes, places, blocks, left)

    def step(real, imag, parts):
        with_real, with_imag = dot(left[...], real), dot(left[...], imag)
        for part, at in parts:
            here = pl.ds(at, mine.shape[1] // (sizes[0] // 2))
            out[0, :, here] = with_real[:, part]
            out[1, :, here] = with_imag[:, part]

    over_columns(sizes, mine, other, step)


def imag_rows_kernel(sizes, places, mine, other, so_far, *refs):
    blocks, (out, left, wide, sem) = refs[:-4], refs[-4:]
    rows_in_order(sizes, places, blocks, left)
    group = mine.shape[1] // (sizes[0] // 2)

    def copy(at):
        return pltpu.make_async_copy(wide.at[:, :, pl.ds(at, group)], out.at[:, :, pl.ds(at, group)], sem.at[at // group])

    def step(real, imag, parts):
        with_real, with_imag = dot(left[...], real), dot(left[...], imag)
        for part, at in parts:
            here = pl.ds(at, group)
            wide[0, :, here] = so_far[0, :, here] + with_imag[:, part]
            wide[1, :, here] = so_far[1, :, here] - with_real[:, part]
            copy(at).start()

    over_columns(sizes, mine, other, step)

    @pl.loop(0, out.shape[2] // group)
    def _(i):
        copy(pl.multiple_of(i * group, group)).wait()


def solution(mesh):
    sizes = tuple(mesh.shape[axis] for axis in AXES)
    rows, cols, slabs = sizes
    half = cols // 2

    def exchange(array, dr, dc, ds):
        pairs = []
        for r in range(rows):
            for c in range(cols):
                for s in range(slabs):
                    pairs.append(((r * cols + c) * slabs + s, ((r ^ dr) * cols + (c ^ dc)) * slabs + (s ^ ds)))
        return lax.ppermute(array, AXES, pairs)

    def body(fields):
        _, size, pixels = fields.shape
        out_rows, out_cols = half * slabs * size, rows * slabs * size
        part_shape = pltpu.VMEM((size, pixels), fields.dtype)

        def call(kernel, out_shape, arrays, scratch=(), specs=None, flops=0, out_spec=VMEM):
            return pl.pallas_call(
                kernel,
                out_shape=out_shape,
                in_specs=specs or [VMEM] * len(arrays),
                out_specs=jax.tree.map(lambda _: out_spec, out_shape),
                scratch_shapes=scratch,
                compiler_params=PARAMS,
                cost_estimate=weight(flops),
            )(*(arrays if specs else in_vmem(arrays)))

        own = call(
            split_kernel, [part_shape] * 2, [pltpu.with_memory_space_constraint(fields, pltpu.HBM)],
            [pltpu.SemaphoreType.DMA((2,))], [ANY],
        )
        blocks, offsets = [fields], [(0, 0)]
        steps = [(0, 1)]
        bit = rows // 2
        while bit > 1:
            steps.append((bit, 0))
            bit //= 2
        for dr, ds in steps:
            blocks = blocks + [exchange(block, dr, 0, ds) for block in blocks]
            offsets = offsets + [(a ^ dr, b ^ ds) for a, b in offsets]
        mine = call(
            functools.partial(order_kernel, sizes, offsets),
            pltpu.VMEM((2, out_cols // 2, pixels), fields.dtype), [*own, *blocks[1:]],
        )
        other = exchange(mine, 1, 0, 0)
        places = [(shift, turn) for shift in range(half) for turn in range(slabs)]
        slots = []
        for i, part in enumerate(own):
            if i > 0:
                part = call(relay_kernel, part_shape, [part, blocks[1]])
            far = exchange(part, 0, half, 0)
            keep, give = call(functools.partial(choose_kernel, sizes), [part_shape] * 2, [part, far], flops=EARLY)
            got = [keep]
            for shift, turn in places[1:]:
                got.append(exchange(give if turn else keep, 0, shift, turn))
            slots.append(got)
        left = pltpu.VMEM((out_rows, pixels), fields.dtype)
        so_far = call(
            functools.partial(real_rows_kernel, sizes, places),
            pltpu.VMEM((2, out_rows, out_cols), jnp.float32), [mine, other, *slots[0]], [left], flops=MIDDLE,
        )
        return call(
            functools.partial(imag_rows_kernel, sizes, places),
            jax.ShapeDtypeStruct((2, out_rows, out_cols), jnp.float32), [mine, other, so_far, *slots[1]],
            [left, pltpu.VMEM((2, out_rows, out_cols), jnp.float32), pltpu.SemaphoreType.DMA((rows,))], out_spec=ANY,
        )

    placed = (P(None, AXES, None),)
    return jax.shard_map(
        body, mesh=mesh, in_specs=placed, out_specs=P(None, ("row", "slab"), "col"), check_vma=False
    )
```

```python
import functools

import jax
import jax.numpy as jnp
from jax import lax
from jax.experimental import pallas as pl
from jax.experimental.pallas import tpu as pltpu
from jax.sharding import PartitionSpec as P

AXES = ("row", "col", "slab")
TILE = 256
ANY = pl.BlockSpec(memory_space=pl.ANY)
VMEM = pl.BlockSpec(memory_space=pltpu.VMEM)
PARAMS = pltpu.CompilerParams(vmem_limit_bytes=24 * 1024 * 1024)
EARLY, MIDDLE, LIGHT = 30_000_000_000, 10_000_000_000, 1_000_000_000


def weight(flops):
    return pl.CostEstimate(flops=flops, bytes_accessed=1 << 18, transcendentals=0) if flops else None


def dot(left, right):
    return lax.dot_general(left, right, (((1,), (1,)), ((), ())), preferred_element_type=jnp.float32)


def in_vmem(arrays):
    return [pltpu.with_memory_space_constraint(array, pltpu.VMEM) for array in arrays]


def split_kernel(fields, *refs):
    outs, sems = refs[:-1], refs[-1]
    copies = [pltpu.make_async_copy(fields.at[i], out, sems.at[i]) for i, out in enumerate(outs)]
    for copy in copies:
        copy.start()
    for copy in copies:
        copy.wait()


def relay_kernel(part, out):
    out[...] = part[...]


def choose_kernel(sizes, own, far, keep, give):
    near = lax.div(lax.axis_index("col"), sizes[1] // 2) == lax.axis_index("slab")
    keep[...] = jnp.where(near, own[...], far[...])
    give[...] = jnp.where(near, far[...], own[...])


def order_kernel(sizes, offsets, own_real, own_imag, *refs):
    r, s = lax.axis_index("row"), lax.axis_index("slab")
    cols, mine = refs[:-1], refs[-1]
    size = own_real.shape[0]

    def place(dr, ds):
        at = lax.div(lax.bitwise_xor(r, dr), 2) * sizes[2] + lax.bitwise_xor(s, ds)
        return pl.ds(pl.multiple_of(at * size, size), size)

    for i, own in enumerate((own_real, own_imag)):
        mine[i, place(0, 0)] = own[...]
    for ref, (dr, ds) in zip(cols, offsets[1:]):
        mine[:, place(dr, ds)] = ref[...]


def rows_in_order(sizes, places, refs, left):
    c, s = lax.axis_index("col"), lax.axis_index("slab")
    for ref, (shift, turn) in zip(refs, places):
        size = ref.shape[0]
        at = lax.rem(lax.bitwise_xor(c, shift), sizes[1] // 2) * sizes[2] + lax.bitwise_xor(s, turn)
        left[pl.ds(pl.multiple_of(at * size, size), size)] = ref[...]


def over_columns(sizes, mine, other, step):
    group = mine.shape[1] // (sizes[0] // 2)
    core = lax.rem(lax.axis_index("row"), 2)
    for cols, which in ((mine, core), (other, 1 - core)):

        @pl.loop(0, mine.shape[1] // TILE)
        def _(tile):
            here = pl.ds(pl.multiple_of(tile * TILE, TILE), TILE)
            parts = []
            for i in range(TILE // group):
                at = (2 * (tile * (TILE // group) + i) + which) * group
                parts.append((slice(i * group, (i + 1) * group), pl.multiple_of(at, group)))
            step(cols[0, here], cols[1, here], parts)


def real_rows_kernel(sizes, places, mine, other, *refs):
    blocks, out, left = refs[:-2], refs[-2], refs[-1]
    rows_in_order(sizes, places, blocks, left)

    def step(real, imag, parts):
        with_real, with_imag = dot(left[...], real), dot(left[...], imag)
        for part, at in parts:
            here = pl.ds(at, mine.shape[1] // (sizes[0] // 2))
            out[0, :, here] = with_real[:, part]
            out[1, :, here] = with_imag[:, part]

    over_columns(sizes, mine, other, step)


def imag_rows_kernel(sizes, places, mine, other, so_far, *refs):
    blocks, (out, left, wide, sem) = refs[:-4], refs[-4:]
    rows_in_order(sizes, places, blocks, left)
    group = mine.shape[1] // (sizes[0] // 2)

    def copy(at):
        return pltpu.make_async_copy(wide.at[:, :, pl.ds(at, group)], out.at[:, :, pl.ds(at, group)], sem.at[at // group])

    def step(real, imag, parts):
        with_real, with_imag = dot(left[...], real), dot(left[...], imag)
        for part, at in parts:
            here = pl.ds(at, group)
            wide[0, :, here] = so_far[0, :, here] + with_imag[:, part]
            wide[1, :, here] = so_far[1, :, here] - with_real[:, part]
            copy(at).start()

    over_columns(sizes, mine, other, step)

    @pl.loop(0, out.shape[2] // group)
    def _(i):
        copy(pl.multiple_of(i * group, group)).wait()


def solution(mesh):
    sizes = tuple(mesh.shape[axis] for axis in AXES)
    rows, cols, slabs = sizes
    half = cols // 2

    def exchange(array, dr, dc, ds):
        pairs = []
        for r in range(rows):
            for c in range(cols):
                for s in range(slabs):
                    pairs.append(((r * cols + c) * slabs + s, ((r ^ dr) * cols + (c ^ dc)) * slabs + (s ^ ds)))
        return lax.ppermute(array, AXES, pairs)

    def body(fields):
        _, size, pixels = fields.shape
        out_rows, out_cols = half * slabs * size, rows * slabs * size
        part_shape = pltpu.VMEM((size, pixels), fields.dtype)

        def call(kernel, out_shape, arrays, scratch=(), specs=None, flops=0, out_spec=VMEM):
            return pl.pallas_call(
                kernel,
                out_shape=out_shape,
                in_specs=specs or [VMEM] * len(arrays),
                out_specs=jax.tree.map(lambda _: out_spec, out_shape),
                scratch_shapes=scratch,
                compiler_params=PARAMS,
                cost_estimate=weight(flops),
            )(*(arrays if specs else in_vmem(arrays)))

        own = call(
            split_kernel, [part_shape] * 2, [pltpu.with_memory_space_constraint(fields, pltpu.HBM)],
            [pltpu.SemaphoreType.DMA((2,))], [ANY],
        )
        blocks, offsets = [fields], [(0, 0)]
        steps = [(0, 1)]
        bit = rows // 2
        while bit > 1:
            steps.append((bit, 0))
            bit //= 2
        for dr, ds in steps:
            blocks = blocks + [exchange(block, dr, 0, ds) for block in blocks]
            offsets = offsets + [(a ^ dr, b ^ ds) for a, b in offsets]
        mine = call(
            functools.partial(order_kernel, sizes, offsets),
            pltpu.VMEM((2, out_cols // 2, pixels), fields.dtype), [*own, *blocks[1:]],
        )
        other = exchange(mine, 1, 0, 0)
        places = [(shift, turn) for shift in range(half) for turn in range(slabs)]
        slots = []
        for i, part in enumerate(own):
            far = exchange(part, 0, half, 0)
            if i == 0:
                far = call(relay_kernel, part_shape, [far], flops=LIGHT)
            keep, give = call(functools.partial(choose_kernel, sizes), [part_shape] * 2, [part, far], flops=EARLY if i else LIGHT)
            got = [keep]
            for shift, turn in places[1:]:
                got.append(exchange(give if turn else keep, 0, shift, turn))
            slots.append(got)
        left = pltpu.VMEM((out_rows, pixels), fields.dtype)
        so_far = call(
            functools.partial(real_rows_kernel, sizes, places),
            pltpu.VMEM((2, out_rows, out_cols), jnp.float32), [mine, other, *slots[0]], [left], flops=MIDDLE,
        )
        return call(
            functools.partial(imag_rows_kernel, sizes, places),
            jax.ShapeDtypeStruct((2, out_rows, out_cols), jnp.float32), [mine, other, so_far, *slots[1]],
            [left, pltpu.VMEM((2, out_rows, out_cols), jnp.float32), pltpu.SemaphoreType.DMA((rows,))], out_spec=ANY,
        )

    placed = (P(None, AXES, None),)
    return jax.shard_map(
        body, mesh=mesh, in_specs=placed, out_specs=P(None, ("row", "slab"), "col"), check_vma=False
    )
```

```python
import functools

import jax
import jax.numpy as jnp
from jax import lax
from jax.experimental import pallas as pl
from jax.experimental.pallas import tpu as pltpu
from jax.sharding import PartitionSpec as P

AXES = ("row", "col", "slab")
TILE = 256
ANY = pl.BlockSpec(memory_space=pl.ANY)
VMEM = pl.BlockSpec(memory_space=pltpu.VMEM)
PARAMS = pltpu.CompilerParams(vmem_limit_bytes=24 * 1024 * 1024)
EARLY, MIDDLE, LIGHT = 30_000_000_000, 10_000_000_000, 1_000_000_000


def weight(flops):
    return pl.CostEstimate(flops=flops, bytes_accessed=1 << 18, transcendentals=0) if flops else None


def dot(left, right):
    return lax.dot_general(left, right, (((1,), (1,)), ((), ())), preferred_element_type=jnp.float32)


def in_vmem(arrays):
    return [pltpu.with_memory_space_constraint(array, pltpu.VMEM) for array in arrays]


def split_kernel(fields, *refs):
    outs, sems = refs[:-1], refs[-1]
    copies = [pltpu.make_async_copy(fields.at[i], out, sems.at[i]) for i, out in enumerate(outs)]
    for copy in copies:
        copy.start()
    for copy in copies:
        copy.wait()


def relay_kernel(part, out):
    out[...] = part[...]


def choose_kernel(sizes, own, far, keep, give):
    near = lax.div(lax.axis_index("col"), sizes[1] // 2) == lax.axis_index("slab")
    keep[...] = jnp.where(near, own[...], far[...])
    give[...] = jnp.where(near, far[...], own[...])


def order_kernel(sizes, offsets, own_real, own_imag, *refs):
    r, s = lax.axis_index("row"), lax.axis_index("slab")
    cols, mine = refs[:-1], refs[-1]
    size = own_real.shape[0]

    def place(dr, ds):
        at = lax.div(lax.bitwise_xor(r, dr), 2) * sizes[2] + lax.bitwise_xor(s, ds)
        return pl.ds(pl.multiple_of(at * size, size), size)

    for i, own in enumerate((own_real, own_imag)):
        mine[i, place(0, 0)] = own[...]
    for ref, (dr, ds) in zip(cols, offsets[1:]):
        mine[:, place(dr, ds)] = ref[...]


def rows_in_order(sizes, places, refs, left):
    c, s = lax.axis_index("col"), lax.axis_index("slab")
    for ref, (shift, turn) in zip(refs, places):
        size = ref.shape[0]
        at = lax.rem(lax.bitwise_xor(c, shift), sizes[1] // 2) * sizes[2] + lax.bitwise_xor(s, turn)
        left[pl.ds(pl.multiple_of(at * size, size), size)] = ref[...]


def over_columns(sizes, mine, other, step):
    group = mine.shape[1] // (sizes[0] // 2)
    core = lax.rem(lax.axis_index("row"), 2)
    for cols, which in ((mine, core), (other, 1 - core)):

        def one_tile(tile, cols=cols, which=which):
            here = pl.ds(tile * TILE if isinstance(tile, int) else pl.multiple_of(tile * TILE, TILE), TILE)
            parts = []
            for i in range(TILE // group):
                at = (2 * (tile * (TILE // group) + i) + which) * group
                parts.append((slice(i * group, (i + 1) * group), pl.multiple_of(at, group)))
            step(cols[0, here], cols[1, here], parts)

        if mine.shape[1] == TILE:
            one_tile(0)
        else:
            pl.loop(0, mine.shape[1] // TILE)(one_tile)


def real_rows_kernel(sizes, places, mine, other, *refs):
    blocks, out, left = refs[:-2], refs[-2], refs[-1]
    rows_in_order(sizes, places, blocks, left)

    def step(real, imag, parts):
        with_real, with_imag = dot(left[...], real), dot(left[...], imag)
        for part, at in parts:
            here = pl.ds(at, mine.shape[1] // (sizes[0] // 2))
            out[0, :, here] = with_real[:, part]
            out[1, :, here] = with_imag[:, part]

    over_columns(sizes, mine, other, step)


def imag_rows_kernel(sizes, places, mine, other, so_far, *refs):
    blocks, (out, left, wide, sem) = refs[:-4], refs[-4:]
    rows_in_order(sizes, places, blocks, left)
    group = mine.shape[1] // (sizes[0] // 2)

    def copy(at):
        return pltpu.make_async_copy(wide.at[:, :, pl.ds(at, group)], out.at[:, :, pl.ds(at, group)], sem.at[at // group])

    def step(real, imag, parts):
        with_real, with_imag = dot(left[...], real), dot(left[...], imag)
        for part, at in parts:
            here = pl.ds(at, group)
            wide[0, :, here] = so_far[0, :, here] + with_imag[:, part]
            wide[1, :, here] = so_far[1, :, here] - with_real[:, part]
            copy(at).start()

    over_columns(sizes, mine, other, step)

    @pl.loop(0, out.shape[2] // group)
    def _(i):
        copy(pl.multiple_of(i * group, group)).wait()


def solution(mesh):
    sizes = tuple(mesh.shape[axis] for axis in AXES)
    rows, cols, slabs = sizes
    half = cols // 2

    def exchange(array, dr, dc, ds):
        pairs = []
        for r in range(rows):
            for c in range(cols):
                for s in range(slabs):
                    pairs.append(((r * cols + c) * slabs + s, ((r ^ dr) * cols + (c ^ dc)) * slabs + (s ^ ds)))
        return lax.ppermute(array, AXES, pairs)

    def body(fields):
        _, size, pixels = fields.shape
        out_rows, out_cols = half * slabs * size, rows * slabs * size
        part_shape = pltpu.VMEM((size, pixels), fields.dtype)

        def call(kernel, out_shape, arrays, scratch=(), specs=None, flops=0, out_spec=VMEM):
            return pl.pallas_call(
                kernel,
                out_shape=out_shape,
                in_specs=specs or [VMEM] * len(arrays),
                out_specs=jax.tree.map(lambda _: out_spec, out_shape),
                scratch_shapes=scratch,
                compiler_params=PARAMS,
                cost_estimate=weight(flops),
            )(*(arrays if specs else in_vmem(arrays)))

        own = call(
            split_kernel, [part_shape] * 2, [pltpu.with_memory_space_constraint(fields, pltpu.HBM)],
            [pltpu.SemaphoreType.DMA((2,))], [ANY],
        )
        blocks, offsets = [fields], [(0, 0)]
        steps = [(0, 1)]
        bit = rows // 2
        while bit > 1:
            steps.append((bit, 0))
            bit //= 2
        for dr, ds in steps:
            blocks = blocks + [exchange(block, dr, 0, ds) for block in blocks]
            offsets = offsets + [(a ^ dr, b ^ ds) for a, b in offsets]
        mine = call(
            functools.partial(order_kernel, sizes, offsets),
            pltpu.VMEM((2, out_cols // 2, pixels), fields.dtype), [*own, *blocks[1:]],
        )
        other = exchange(mine, 1, 0, 0)
        places = [(shift, turn) for shift in range(half) for turn in range(slabs)]
        slots = []
        for i, part in enumerate(own):
            far = exchange(part, 0, half, 0)
            if i == 0:
                far = call(relay_kernel, part_shape, [far], flops=LIGHT)
            keep, give = call(functools.partial(choose_kernel, sizes), [part_shape] * 2, [part, far], flops=EARLY if i else LIGHT)
            got = [keep]
            for shift, turn in places[1:]:
                got.append(exchange(give if turn else keep, 0, shift, turn))
            slots.append(got)
        left = pltpu.VMEM((out_rows, pixels), fields.dtype)
        so_far = call(
            functools.partial(real_rows_kernel, sizes, places),
            pltpu.VMEM((2, out_rows, out_cols), jnp.float32), [mine, other, *slots[0]], [left], flops=MIDDLE,
        )
        return call(
            functools.partial(imag_rows_kernel, sizes, places),
            jax.ShapeDtypeStruct((2, out_rows, out_cols), jnp.float32), [mine, other, so_far, *slots[1]],
            [left, pltpu.VMEM((2, out_rows, out_cols), jnp.float32), pltpu.SemaphoreType.DMA((rows,))], out_spec=ANY,
        )

    placed = (P(None, AXES, None),)
    return jax.shard_map(
        body, mesh=mesh, in_specs=placed, out_specs=P(None, ("row", "slab"), "col"), check_vma=False
    )
```

```python
import functools

import jax
import jax.numpy as jnp
from jax import lax
from jax.experimental import pallas as pl
from jax.experimental.pallas import tpu as pltpu
from jax.sharding import PartitionSpec as P

AXES = ("row", "col", "slab")
TILE = 256
ANY = pl.BlockSpec(memory_space=pl.ANY)
VMEM = pl.BlockSpec(memory_space=pltpu.VMEM)
PARAMS = pltpu.CompilerParams(vmem_limit_bytes=24 * 1024 * 1024)
EARLY, MIDDLE = 30_000_000_000, 5_000_000_000


def weight(flops):
    return pl.CostEstimate(flops=flops, bytes_accessed=1 << 18, transcendentals=0) if flops else None


def dot(left, right):
    return lax.dot_general(left, right, (((1,), (1,)), ((), ())), preferred_element_type=jnp.float32)


def in_vmem(arrays):
    return [pltpu.with_memory_space_constraint(array, pltpu.VMEM) for array in arrays]


def split_kernel(starts, fields, *refs):
    outs, sems = refs[:-1], refs[-1]
    copies = [
        pltpu.make_async_copy(fields.at[:, :, pl.ds(at, out.shape[2])], out, sems.at[i])
        for i, (at, out) in enumerate(zip(starts, outs))
    ]
    for copy in copies:
        copy.start()
    for copy in copies:
        copy.wait()


def relay_kernel(part, *refs):
    out = refs[-1]
    out[...] = part[...]


def choose_kernel(sizes, own, far, keep, give):
    near = lax.div(lax.axis_index("col"), sizes[1] // 2) == lax.axis_index("slab")
    keep[...] = jnp.where(near, own[...], far[...])
    give[...] = jnp.where(near, far[...], own[...])


def order_kernel(sizes, offsets, starts, *refs):
    r, s = lax.axis_index("row"), lax.axis_index("slab")
    own, cols, mine = refs[: len(starts)], refs[len(starts) : -1], refs[-1]
    size = own[0].shape[1]

    def place(dr, ds):
        at = lax.div(lax.bitwise_xor(r, dr), 2) * sizes[2] + lax.bitwise_xor(s, ds)
        return pl.ds(pl.multiple_of(at * size, size), size)

    for start, part in zip(starts, own):
        mine[:, place(0, 0), start : start + part.shape[2]] = part[...]
    for ref, (dr, ds) in zip(cols, offsets[1:]):
        mine[:, place(dr, ds)] = ref[...]


def rows_in_order(sizes, places, refs, left):
    c, s = lax.axis_index("col"), lax.axis_index("slab")
    for ref, (shift, turn) in zip(refs, places):
        size = ref.shape[1]
        at = lax.rem(lax.bitwise_xor(c, shift), sizes[1] // 2) * sizes[2] + lax.bitwise_xor(s, turn)
        left[:, pl.ds(pl.multiple_of(at * size, size), size)] = ref[...]


def over_columns(sizes, start, left, mine, other, step):
    group = mine.shape[1] // (sizes[0] // 2)
    core = lax.rem(lax.axis_index("row"), 2)
    pixels = pl.ds(start, left.shape[2])
    for cols, which in ((mine, core), (other, 1 - core)):

        @pl.loop(0, mine.shape[1] // TILE)
        def _(tile):
            here = pl.ds(pl.multiple_of(tile * TILE, TILE), TILE)
            c_real, c_imag = cols[0, here, pixels], cols[1, here, pixels]
            real = dot(left[0], c_real) + dot(left[1], c_imag)
            imag = dot(left[0], c_imag) - dot(left[1], c_real)
            for i in range(TILE // group):
                at = pl.multiple_of((2 * (tile * (TILE // group) + i) + which) * group, group)
                step(pl.ds(at, group), at, real[:, i * group : (i + 1) * group], imag[:, i * group : (i + 1) * group])


def middle_kernel(sizes, places, start, first, mine, other, *refs):
    so_far, blocks, (out, left) = (None if first else refs[0]), refs[0 if first else 1 : -2], refs[-2:]
    rows_in_order(sizes, places, blocks, left)

    def step(here, at, real, imag):
        out[0, :, here] = real if first else so_far[0, :, here] + real
        out[1, :, here] = imag if first else so_far[1, :, here] + imag

    over_columns(sizes, start, left, mine, other, step)


def last_kernel(sizes, places, start, mine, other, so_far, *refs):
    blocks, (out, left, wide, sem) = refs[:-4], refs[-4:]
    rows_in_order(sizes, places, blocks, left)
    group = mine.shape[1] // (sizes[0] // 2)

    def copy(at):
        return pltpu.make_async_copy(wide.at[:, :, pl.ds(at, group)], out.at[:, :, pl.ds(at, group)], sem.at[at // group])

    def step(here, at, real, imag):
        wide[0, :, here] = so_far[0, :, here] + real
        wide[1, :, here] = so_far[1, :, here] + imag
        copy(at).start()

    over_columns(sizes, start, left, mine, other, step)

    @pl.loop(0, out.shape[2] // group)
    def _(i):
        copy(pl.multiple_of(i * group, group)).wait()


def solution(mesh):
    sizes = tuple(mesh.shape[axis] for axis in AXES)
    rows, cols, slabs = sizes
    half = cols // 2

    def exchange(array, dr, dc, ds):
        pairs = []
        for r in range(rows):
            for c in range(cols):
                for s in range(slabs):
                    pairs.append(((r * cols + c) * slabs + s, ((r ^ dr) * cols + (c ^ dc)) * slabs + (s ^ ds)))
        return lax.ppermute(array, AXES, pairs)

    def body(fields):
        _, size, pixels = fields.shape
        out_rows, out_cols = half * slabs * size, rows * slabs * size
        parts = [pixels // 2] * 2
        starts = [sum(parts[:i]) for i in range(len(parts))]
        shapes = [pltpu.VMEM((2, size, p), fields.dtype) for p in parts]

        def call(kernel, out_shape, arrays, scratch=(), specs=None, flops=0, out_spec=VMEM):
            return pl.pallas_call(
                kernel,
                out_shape=out_shape,
                in_specs=specs or [VMEM] * len(arrays),
                out_specs=jax.tree.map(lambda _: out_spec, out_shape),
                scratch_shapes=scratch,
                compiler_params=PARAMS,
                cost_estimate=weight(flops),
            )(*(arrays if specs else in_vmem(arrays)))

        own = call(
            functools.partial(split_kernel, starts), shapes, [pltpu.with_memory_space_constraint(fields, pltpu.HBM)],
            [pltpu.SemaphoreType.DMA((len(parts),))], [ANY],
        )
        blocks, offsets = [fields], [(0, 0)]
        steps = [(0, 1)]
        bit = rows // 2
        while bit > 1:
            steps.append((bit, 0))
            bit //= 2
        for dr, ds in steps:
            blocks = blocks + [exchange(block, dr, 0, ds) for block in blocks]
            offsets = offsets + [(a ^ dr, b ^ ds) for a, b in offsets]
        mine = call(
            functools.partial(order_kernel, sizes, offsets, starts),
            pltpu.VMEM((2, out_cols // 2, pixels), fields.dtype), [*own, *blocks[1:]],
        )
        other = exchange(mine, 1, 0, 0)
        places = [(shift, turn) for shift in range(half) for turn in range(slabs)]
        slots = []
        for i, part in enumerate(own):
            if i > 0:
                part = call(relay_kernel, shapes[i], [part, blocks[1]])
            far = exchange(part, 0, half, 0)
            keep, give = call(functools.partial(choose_kernel, sizes), [shapes[i]] * 2, [part, far], flops=EARLY)
            got = [keep]
            for shift, turn in places[1:]:
                got.append(exchange(give if turn else keep, 0, shift, turn))
            slots.append(got)
        so_far = []
        for i in range(len(parts) - 1):
            so_far = [
                call(
                    functools.partial(middle_kernel, sizes, places, starts[i], i == 0),
                    pltpu.VMEM((2, out_rows, out_cols), jnp.float32), [mine, other, *so_far, *slots[i]],
                    [pltpu.VMEM((2, out_rows, parts[i]), fields.dtype)], flops=MIDDLE,
                )
            ]
        return call(
            functools.partial(last_kernel, sizes, places, starts[-1]),
            jax.ShapeDtypeStruct((2, out_rows, out_cols), jnp.float32), [mine, other, *so_far, *slots[-1]],
            [
                pltpu.VMEM((2, out_rows, parts[-1]), fields.dtype),
                pltpu.VMEM((2, out_rows, out_cols), jnp.float32),
                pltpu.SemaphoreType.DMA((rows,)),
            ],
            out_spec=ANY,
        )

    placed = (P(None, AXES, None),)
    return jax.shard_map(
        body, mesh=mesh, in_specs=placed, out_specs=P(None, ("row", "slab"), "col"), check_vma=False
    )
```

```python
import functools

import jax
import jax.numpy as jnp
from jax import lax
from jax.experimental import pallas as pl
from jax.experimental.pallas import tpu as pltpu
from jax.sharding import PartitionSpec as P

AXES = ("row", "col", "slab")
TILE = 256
ANY = pl.BlockSpec(memory_space=pl.ANY)
VMEM = pl.BlockSpec(memory_space=pltpu.VMEM)
PARAMS = pltpu.CompilerParams(vmem_limit_bytes=24 * 1024 * 1024)
EARLY, MIDDLE, LIGHT = 30_000_000_000, 10_000_000_000, 1_000_000_000


def weight(flops):
    return pl.CostEstimate(flops=flops, bytes_accessed=1 << 18, transcendentals=0) if flops else None


def dot(left, right):
    return lax.dot_general(left, right, (((1,), (1,)), ((), ())), preferred_element_type=jnp.float32)


def in_vmem(arrays):
    return [pltpu.with_memory_space_constraint(array, pltpu.VMEM) for array in arrays]


def split_kernel(starts, fields, *refs):
    outs, sems = refs[:-1], refs[-1]
    copies = [
        pltpu.make_async_copy(fields.at[:, :, pl.ds(at, out.shape[2])], out, sems.at[i])
        for i, (at, out) in enumerate(zip(starts, outs))
    ]
    for copy in copies:
        copy.start()
    for copy in copies:
        copy.wait()


def relay_kernel(part, *refs):
    out = refs[-1]
    out[...] = part[...]


def choose_kernel(sizes, own, far, keep, give):
    near = lax.div(lax.axis_index("col"), sizes[1] // 2) == lax.axis_index("slab")
    keep[...] = jnp.where(near, own[...], far[...])
    give[...] = jnp.where(near, far[...], own[...])


def order_kernel(sizes, offsets, starts, *refs):
    r, s = lax.axis_index("row"), lax.axis_index("slab")
    own, cols, mine = refs[: len(starts)], refs[len(starts) : -1], refs[-1]
    size = own[0].shape[1]

    def place(dr, ds):
        at = lax.div(lax.bitwise_xor(r, dr), 2) * sizes[2] + lax.bitwise_xor(s, ds)
        return pl.ds(pl.multiple_of(at * size, size), size)

    for start, part in zip(starts, own):
        mine[:, place(0, 0), start : start + part.shape[2]] = part[...]
    for ref, (dr, ds) in zip(cols, offsets[1:]):
        mine[:, place(dr, ds)] = ref[...]


def rows_in_order(sizes, places, refs, left):
    c, s = lax.axis_index("col"), lax.axis_index("slab")
    for ref, (shift, turn) in zip(refs, places):
        size = ref.shape[1]
        at = lax.rem(lax.bitwise_xor(c, shift), sizes[1] // 2) * sizes[2] + lax.bitwise_xor(s, turn)
        left[:, pl.ds(pl.multiple_of(at * size, size), size)] = ref[...]


def over_columns(sizes, start, left, mine, other, step):
    group = mine.shape[1] // (sizes[0] // 2)
    core = lax.rem(lax.axis_index("row"), 2)
    pixels = pl.ds(start, left.shape[2])
    for cols, which in ((mine, core), (other, 1 - core)):

        @pl.loop(0, mine.shape[1] // TILE)
        def _(tile):
            here = pl.ds(pl.multiple_of(tile * TILE, TILE), TILE)
            c_real, c_imag = cols[0, here, pixels], cols[1, here, pixels]
            real = dot(left[0], c_real) + dot(left[1], c_imag)
            imag = dot(left[0], c_imag) - dot(left[1], c_real)
            for i in range(TILE // group):
                at = pl.multiple_of((2 * (tile * (TILE // group) + i) + which) * group, group)
                step(pl.ds(at, group), at, real[:, i * group : (i + 1) * group], imag[:, i * group : (i + 1) * group])


def middle_kernel(sizes, places, start, first, mine, other, *refs):
    so_far, blocks, (out, left) = (None if first else refs[0]), refs[0 if first else 1 : -2], refs[-2:]
    rows_in_order(sizes, places, blocks, left)

    def step(here, at, real, imag):
        out[0, :, here] = real if first else so_far[0, :, here] + real
        out[1, :, here] = imag if first else so_far[1, :, here] + imag

    over_columns(sizes, start, left, mine, other, step)


def last_kernel(sizes, places, start, mine, other, so_far, *refs):
    blocks, (out, left, wide, sem) = refs[:-4], refs[-4:]
    rows_in_order(sizes, places, blocks, left)
    group = mine.shape[1] // (sizes[0] // 2)

    def copy(at):
        return pltpu.make_async_copy(wide.at[:, :, pl.ds(at, group)], out.at[:, :, pl.ds(at, group)], sem.at[at // group])

    def step(here, at, real, imag):
        wide[0, :, here] = so_far[0, :, here] + real
        wide[1, :, here] = so_far[1, :, here] + imag
        copy(at).start()

    over_columns(sizes, start, left, mine, other, step)

    @pl.loop(0, out.shape[2] // group)
    def _(i):
        copy(pl.multiple_of(i * group, group)).wait()


def solution(mesh):
    sizes = tuple(mesh.shape[axis] for axis in AXES)
    rows, cols, slabs = sizes
    half = cols // 2

    def exchange(array, dr, dc, ds):
        pairs = []
        for r in range(rows):
            for c in range(cols):
                for s in range(slabs):
                    pairs.append(((r * cols + c) * slabs + s, ((r ^ dr) * cols + (c ^ dc)) * slabs + (s ^ ds)))
        return lax.ppermute(array, AXES, pairs)

    def body(fields):
        _, size, pixels = fields.shape
        out_rows, out_cols = half * slabs * size, rows * slabs * size
        parts = [pixels // 2] * 2
        starts = [sum(parts[:i]) for i in range(len(parts))]
        shapes = [pltpu.VMEM((2, size, p), fields.dtype) for p in parts]

        def call(kernel, out_shape, arrays, scratch=(), specs=None, flops=0, out_spec=VMEM):
            return pl.pallas_call(
                kernel,
                out_shape=out_shape,
                in_specs=specs or [VMEM] * len(arrays),
                out_specs=jax.tree.map(lambda _: out_spec, out_shape),
                scratch_shapes=scratch,
                compiler_params=PARAMS,
                cost_estimate=weight(flops),
            )(*(arrays if specs else in_vmem(arrays)))

        own = call(
            functools.partial(split_kernel, starts), shapes, [pltpu.with_memory_space_constraint(fields, pltpu.HBM)],
            [pltpu.SemaphoreType.DMA((len(parts),))], [ANY],
        )
        blocks, offsets = [fields], [(0, 0)]
        steps = [(0, 1)]
        bit = rows // 2
        while bit > 1:
            steps.append((bit, 0))
            bit //= 2
        for dr, ds in steps:
            blocks = blocks + [exchange(block, dr, 0, ds) for block in blocks]
            offsets = offsets + [(a ^ dr, b ^ ds) for a, b in offsets]
        mine = call(
            functools.partial(order_kernel, sizes, offsets, starts),
            pltpu.VMEM((2, out_cols // 2, pixels), fields.dtype), [*own, *blocks[1:]],
        )
        other = exchange(mine, 1, 0, 0)
        places = [(shift, turn) for shift in range(half) for turn in range(slabs)]
        slots = []
        for i, part in enumerate(own):
            far = exchange(part, 0, half, 0)
            if i == 0:
                far = call(relay_kernel, shapes[i], [far], flops=LIGHT)
            keep, give = call(functools.partial(choose_kernel, sizes), [shapes[i]] * 2, [part, far], flops=EARLY if i else LIGHT)
            got = [keep]
            for shift, turn in places[1:]:
                got.append(exchange(give if turn else keep, 0, shift, turn))
            slots.append(got)
        so_far = []
        for i in range(len(parts) - 1):
            so_far = [
                call(
                    functools.partial(middle_kernel, sizes, places, starts[i], i == 0),
                    pltpu.VMEM((2, out_rows, out_cols), jnp.float32), [mine, other, *so_far, *slots[i]],
                    [pltpu.VMEM((2, out_rows, parts[i]), fields.dtype)], flops=MIDDLE,
                )
            ]
        return call(
            functools.partial(last_kernel, sizes, places, starts[-1]),
            jax.ShapeDtypeStruct((2, out_rows, out_cols), jnp.float32), [mine, other, *so_far, *slots[-1]],
            [
                pltpu.VMEM((2, out_rows, parts[-1]), fields.dtype),
                pltpu.VMEM((2, out_rows, out_cols), jnp.float32),
                pltpu.SemaphoreType.DMA((rows,)),
            ],
            out_spec=ANY,
        )

    placed = (P(None, AXES, None),)
    return jax.shard_map(
        body, mesh=mesh, in_specs=placed, out_specs=P(None, ("row", "slab"), "col"), check_vma=False
    )
```

```python
import functools

import jax
import jax.numpy as jnp
from jax import lax
from jax.experimental import pallas as pl
from jax.experimental.pallas import tpu as pltpu
from jax.sharding import PartitionSpec as P

AXES = ("row", "col", "slab")
TILE = 256
ANY = pl.BlockSpec(memory_space=pl.ANY)
VMEM = pl.BlockSpec(memory_space=pltpu.VMEM)
PARAMS = pltpu.CompilerParams(vmem_limit_bytes=24 * 1024 * 1024)
EARLY, MIDDLE, LIGHT = 30_000_000_000, 10_000_000_000, 1_000_000_000


def weight(flops):
    return pl.CostEstimate(flops=flops, bytes_accessed=1 << 18, transcendentals=0) if flops else None


def dot(left, right):
    return lax.dot_general(left, right, (((1,), (1,)), ((), ())), preferred_element_type=jnp.float32)


def in_vmem(arrays):
    return [pltpu.with_memory_space_constraint(array, pltpu.VMEM) for array in arrays]


def split_kernel(starts, fields, *refs):
    outs, sems = refs[:-1], refs[-1]
    copies = [
        pltpu.make_async_copy(fields.at[:, :, pl.ds(at, out.shape[2])], out, sems.at[i])
        for i, (at, out) in enumerate(zip(starts, outs))
    ]
    for copy in copies:
        copy.start()
    for copy in copies:
        copy.wait()


def relay_kernel(part, *refs):
    out = refs[-1]
    out[...] = part[...]


def choose_kernel(sizes, own, far, keep, give):
    near = lax.div(lax.axis_index("col"), sizes[1] // 2) == lax.axis_index("slab")
    keep[...] = jnp.where(near, own[...], far[...])
    give[...] = jnp.where(near, far[...], own[...])


def order_kernel(sizes, offsets, starts, *refs):
    r, s = lax.axis_index("row"), lax.axis_index("slab")
    own, cols, mine = refs[: len(starts)], refs[len(starts) : -1], refs[-1]
    size = own[0].shape[1]

    def place(dr, ds):
        at = lax.div(lax.bitwise_xor(r, dr), 2) * sizes[2] + lax.bitwise_xor(s, ds)
        return pl.ds(pl.multiple_of(at * size, size), size)

    for start, part in zip(starts, own):
        mine[:, place(0, 0), start : start + part.shape[2]] = part[...]
    for ref, (dr, ds) in zip(cols, offsets[1:]):
        mine[:, place(dr, ds)] = ref[...]


def rows_in_order(sizes, places, refs, left):
    c, s = lax.axis_index("col"), lax.axis_index("slab")
    for ref, (shift, turn) in zip(refs, places):
        size = ref.shape[1]
        at = lax.rem(lax.bitwise_xor(c, shift), sizes[1] // 2) * sizes[2] + lax.bitwise_xor(s, turn)
        left[:, pl.ds(pl.multiple_of(at * size, size), size)] = ref[...]


def over_columns(sizes, start, left, mine, other, step):
    group = mine.shape[1] // (sizes[0] // 2)
    core = lax.rem(lax.axis_index("row"), 2)
    pixels = pl.ds(start, left.shape[2])
    for cols, which in ((mine, core), (other, 1 - core)):

        def one_tile(tile, cols=cols, which=which):
            here = pl.ds(tile * TILE if isinstance(tile, int) else pl.multiple_of(tile * TILE, TILE), TILE)
            c_real, c_imag = cols[0, here, pixels], cols[1, here, pixels]
            real = dot(left[0], c_real) + dot(left[1], c_imag)
            imag = dot(left[0], c_imag) - dot(left[1], c_real)
            for i in range(TILE // group):
                at = pl.multiple_of((2 * (tile * (TILE // group) + i) + which) * group, group)
                step(pl.ds(at, group), at, real[:, i * group : (i + 1) * group], imag[:, i * group : (i + 1) * group])

        if mine.shape[1] == TILE:
            one_tile(0)
        else:
            pl.loop(0, mine.shape[1] // TILE)(one_tile)


def middle_kernel(sizes, places, start, first, mine, other, *refs):
    so_far, blocks, (out, left) = (None if first else refs[0]), refs[0 if first else 1 : -2], refs[-2:]
    rows_in_order(sizes, places, blocks, left)

    def step(here, at, real, imag):
        out[0, :, here] = real if first else so_far[0, :, here] + real
        out[1, :, here] = imag if first else so_far[1, :, here] + imag

    over_columns(sizes, start, left, mine, other, step)


def last_kernel(sizes, places, start, mine, other, so_far, *refs):
    blocks, (out, left, wide, sem) = refs[:-4], refs[-4:]
    rows_in_order(sizes, places, blocks, left)
    group = mine.shape[1] // (sizes[0] // 2)

    def copy(at):
        return pltpu.make_async_copy(wide.at[:, :, pl.ds(at, group)], out.at[:, :, pl.ds(at, group)], sem.at[at // group])

    def step(here, at, real, imag):
        wide[0, :, here] = so_far[0, :, here] + real
        wide[1, :, here] = so_far[1, :, here] + imag
        copy(at).start()

    over_columns(sizes, start, left, mine, other, step)

    @pl.loop(0, out.shape[2] // group)
    def _(i):
        copy(pl.multiple_of(i * group, group)).wait()


def solution(mesh):
    sizes = tuple(mesh.shape[axis] for axis in AXES)
    rows, cols, slabs = sizes
    half = cols // 2

    def exchange(array, dr, dc, ds):
        pairs = []
        for r in range(rows):
            for c in range(cols):
                for s in range(slabs):
                    pairs.append(((r * cols + c) * slabs + s, ((r ^ dr) * cols + (c ^ dc)) * slabs + (s ^ ds)))
        return lax.ppermute(array, AXES, pairs)

    def body(fields):
        _, size, pixels = fields.shape
        out_rows, out_cols = half * slabs * size, rows * slabs * size
        parts = [pixels // 2] * 2
        starts = [sum(parts[:i]) for i in range(len(parts))]
        shapes = [pltpu.VMEM((2, size, p), fields.dtype) for p in parts]

        def call(kernel, out_shape, arrays, scratch=(), specs=None, flops=0, out_spec=VMEM):
            return pl.pallas_call(
                kernel,
                out_shape=out_shape,
                in_specs=specs or [VMEM] * len(arrays),
                out_specs=jax.tree.map(lambda _: out_spec, out_shape),
                scratch_shapes=scratch,
                compiler_params=PARAMS,
                cost_estimate=weight(flops),
            )(*(arrays if specs else in_vmem(arrays)))

        own = call(
            functools.partial(split_kernel, starts), shapes, [pltpu.with_memory_space_constraint(fields, pltpu.HBM)],
            [pltpu.SemaphoreType.DMA((len(parts),))], [ANY],
        )
        blocks, offsets = [fields], [(0, 0)]
        steps = [(0, 1)]
        bit = rows // 2
        while bit > 1:
            steps.append((bit, 0))
            bit //= 2
        for dr, ds in steps:
            blocks = blocks + [exchange(block, dr, 0, ds) for block in blocks]
            offsets = offsets + [(a ^ dr, b ^ ds) for a, b in offsets]
        mine = call(
            functools.partial(order_kernel, sizes, offsets, starts),
            pltpu.VMEM((2, out_cols // 2, pixels), fields.dtype), [*own, *blocks[1:]],
        )
        other = exchange(mine, 1, 0, 0)
        places = [(shift, turn) for shift in range(half) for turn in range(slabs)]
        slots = []
        for i, part in enumerate(own):
            far = exchange(part, 0, half, 0)
            if i == 0:
                far = call(relay_kernel, shapes[i], [far], flops=LIGHT)
            keep, give = call(functools.partial(choose_kernel, sizes), [shapes[i]] * 2, [part, far], flops=EARLY if i else LIGHT)
            got = [keep]
            for shift, turn in places[1:]:
                got.append(exchange(give if turn else keep, 0, shift, turn))
            slots.append(got)
        so_far = []
        for i in range(len(parts) - 1):
            so_far = [
                call(
                    functools.partial(middle_kernel, sizes, places, starts[i], i == 0),
                    pltpu.VMEM((2, out_rows, out_cols), jnp.float32), [mine, other, *so_far, *slots[i]],
                    [pltpu.VMEM((2, out_rows, parts[i]), fields.dtype)], flops=MIDDLE,
                )
            ]
        return call(
            functools.partial(last_kernel, sizes, places, starts[-1]),
            jax.ShapeDtypeStruct((2, out_rows, out_cols), jnp.float32), [mine, other, *so_far, *slots[-1]],
            [
                pltpu.VMEM((2, out_rows, parts[-1]), fields.dtype),
                pltpu.VMEM((2, out_rows, out_cols), jnp.float32),
                pltpu.SemaphoreType.DMA((rows,)),
            ],
            out_spec=ANY,
        )

    placed = (P(None, AXES, None),)
    return jax.shard_map(
        body, mesh=mesh, in_specs=placed, out_specs=P(None, ("row", "slab"), "col"), check_vma=False
    )
```
